128 devices in a mesh: dp: 16 (over x, z_hi, core), tensor: 8 (over y, z_lo).
Axes of the slice: x: 4, y: 4, z: 4 (z_hi: 2, z_lo: 2; z = z_hi * 2 + z_lo), core: 2. Of those that a mesh axis runs over, the one named last changes fastest.
Arguments:
- activations: bfloat16 [6144, 4096], P('dp', 'tensor'), may hold values from -6 to 6
- out_grads: bfloat16 [6144, 16384], P('dp', 'tensor'), may hold values from -6 to 6
- basis_in: bfloat16 [4, 1024, 1024], replicated, may hold values from -0.1875 to 0.1875
- basis_out: bfloat16 [16, 1024, 1024], P('tensor'), may hold values from -0.1875 to 0.1875
Outputs:
- scales: float32 [4096, 16384], P('dp', 'tensor')
- natural: bfloat16 [4096, 16384], P('dp', 'tensor')
The draws below stay inside these ranges and needn't reach their ends.
All inputs are finite; a program needn't handle non-finite values.
Results may differ from the reference program's by a relative error of at most 0.015.
Values may be sent and summed in bfloat16 or wider, within the bound.
No kernel may reach another device: no remote copies, remote signals or barrier semaphores. Data moves between devices by JAX's collectives and lax.ppermute only.
A program may use at most 192 MiB of HBM per device.

```python
import math
import jax
import jax.numpy as jnp
from jax import lax

D = 4096
FW = 16384
BLOCK = 1024
TOK_DEV = 384
TOKENS = 6144
N_DP = 16


def raised(values, own_key, source, target, parts, factor):
    def block_of(position):
        return (jnp.arange(values.shape[position]) // (values.shape[position] // parts)).reshape((-1,) + (1,) * (values.ndim - 1 - position))

    near = jax.random.permutation(own_key, parts)[block_of(target)]
    second = (block_of(target) + parts // 2) % parts
    return jnp.where((block_of(source) == near) | (block_of(source) == second), factor * values, values)


def level_of(stream_key, extent, pieces, smallest, largest):
    level, own = 1.0, jax.random.fold_in(stream_key, 6)
    for position, blocks in pieces:
        steps = jnp.exp(jax.random.uniform(jax.random.fold_in(own, position), (blocks,), jnp.float32, smallest / len(pieces), largest / len(pieces)))
        level = level * jnp.repeat(steps, extent[position] // blocks).reshape([-1 if axis == position else 1 for axis in range(len(extent))])
    return level


def gaussian(stream_key, dims, scale, reach, shards=(), kind=jnp.bfloat16):
    drawn = scale * jax.random.normal(stream_key, dims, jnp.float32)
    if shards:
        drawn = drawn * level_of(stream_key, dims, shards, -0.22, 0.18)
    return jnp.clip(drawn, -reach, reach).astype(kind)


def bell_draw_with(own_key, shape, width, reach, cuts, heavy, held_as=jnp.bfloat16):
    drawn = width * jax.random.normal(own_key, shape, jnp.float32)
    if cuts:
        drawn = drawn * level_of(own_key, shape, cuts, -0.22, 0.18)
    return jnp.clip(raised(drawn, jax.random.fold_in(own_key, 3), *heavy), -reach, reach).astype(held_as)


def setup_inputs(seed: int = 0) -> dict:
    key_list = jax.random.split(jax.random.key(seed), 5)
    activations = bell_draw_with(key_list[0], (TOKENS, D), 1.0, 6.0, ((0, 16), (1, 8)), (0, 1, 16, 2.0))
    out_grads = gaussian(key_list[1], (TOKENS, FW), 1.0, 6.0, ((0, 16), (1, 8)))
    basis_in = gaussian(key_list[2], (D // BLOCK, BLOCK, BLOCK), BLOCK ** -0.5, 0.1875)
    basis_out = gaussian(key_list[3], (FW // BLOCK, BLOCK, BLOCK), BLOCK ** -0.5, 0.1875, ((0, 8),))
    return {"activations": activations, "out_grads": out_grads, "basis_in": basis_in, "basis_out": basis_out}


damping = 0.1

def squared(values):
    wide = values.astype(jnp.float32)
    return (wide * wide).astype(jnp.bfloat16)

def contract(left, right):
    return lax.dot_general(left.astype(jnp.float32), right.astype(jnp.float32), (((0,), (0,)), ((), ())))

def reference(activations, out_grads, basis_in, basis_out):
    in_blocks = D // BLOCK
    out_blocks = FW // BLOCK
    rotated_in = jnp.einsum('tbi,bij->tbj', activations.astype(jnp.float32).reshape(TOKENS, in_blocks, BLOCK), basis_in.astype(jnp.float32)).reshape(TOKENS, D).astype(jnp.bfloat16)
    rotated_out = jnp.einsum('tbi,bij->tbj', out_grads.astype(jnp.float32).reshape(TOKENS, out_blocks, BLOCK), basis_out.astype(jnp.float32)).reshape(TOKENS, FW).astype(jnp.bfloat16)

    def group_step(carry, group_index):
        begin = (group_index * TOK_DEV).astype(jnp.int32)
        piece_in = lax.dynamic_slice_in_dim(rotated_in, begin, TOK_DEV, 0)
        piece_out = lax.dynamic_slice_in_dim(rotated_out, begin, TOK_DEV, 0)
        scale_part = lax.optimization_barrier(contract(squared(piece_in), squared(piece_out)).astype(jnp.bfloat16)).astype(jnp.float32)
        grad_part = lax.optimization_barrier(contract(piece_in, piece_out).astype(jnp.bfloat16)).astype(jnp.float32)
        return ((carry[0] + scale_part, carry[1] + grad_part), None)
    zeros = jnp.zeros((D, FW), jnp.float32)
    (scale_sum, grad_sum), _ = lax.scan(group_step, (zeros, zeros), jnp.arange(N_DP, dtype=jnp.int32))
    scales = scale_sum / TOKENS
    rotated = (grad_sum / math.sqrt(TOKENS) / (scales + damping)).astype(jnp.bfloat16)
    half = jnp.einsum('rbj,bij->rbi', rotated.astype(jnp.float32).reshape(D, out_blocks, BLOCK), basis_out.astype(jnp.float32)).reshape(D, FW).astype(jnp.bfloat16)
    natural = jnp.einsum('bij,bjf->bif', basis_in.astype(jnp.float32), half.astype(jnp.float32).reshape(in_blocks, BLOCK, FW)).reshape(D, FW).astype(jnp.bfloat16)
    return (scales, natural)
```

```python
import math

import jax
import jax.numpy as jnp
from jax import lax
from jax.sharding import PartitionSpec as P

damping = 0.1
X = 4
Y = 4


def along_x(v, d):
    pairs = [(i, (i // 4 + d) % X * 4 + i % 4) for i in range(16)]
    return lax.ppermute(v, "dp", pairs)


def along_y(v, d):
    pairs = [(i, (i // 2 + d) % Y * 2 + i % 2) for i in range(8)]
    return lax.ppermute(v, "tensor", pairs)


def swap_dp(v, bit):
    return lax.ppermute(v, "dp", [(i, i ^ bit) for i in range(16)])


def swap_core(v):
    return swap_dp(v, 1)


def swap_z_hi(v):
    return swap_dp(v, 2)


def swap_z_lo(v):
    return lax.ppermute(v, "tensor", [(i, i ^ 1) for i in range(8)])


def transpose_xy(v):
    pairs = []
    for dp in range(16):
        for tensor in range(8):
            x, rest = divmod(dp, 4)
            y, z_lo = divmod(tensor, 2)
            pairs.append((dp * 8 + tensor, (y * 4 + rest) * 8 + x * 2 + z_lo))
    return lax.ppermute(v, ("dp", "tensor"), pairs)


def squared(values):
    wide = values.astype(jnp.float32)
    return (wide * wide).astype(jnp.bfloat16)


def dot(left, right, contract=((1,), (0,))):
    return lax.dot_general(left, right, (contract, ((), ())), preferred_element_type=jnp.float32)


def after(value, *others):
    return lax.optimization_barrier((value,) + others)[0]


def shards(activations, out_grads, basis_in, basis_out):
    tokens, half_in = activations.shape
    block = basis_in.shape[1]
    width = out_grads.shape[1]
    quarter = block // 4
    tokens_all = tokens * 16
    dp = lax.axis_index("dp")
    tensor = lax.axis_index("tensor")
    x = dp // 4
    q = dp % 4
    y = tensor // 2
    z_lo = tensor % 2

    mine = transpose_xy(activations)
    block_basis = lax.dynamic_index_in_dim(basis_in, x, 0, keepdims=False)
    order = [q, q ^ 2, q ^ 1, q ^ 3]
    by_column = jnp.concatenate(
        [lax.dynamic_slice_in_dim(block_basis, k * quarter, quarter, 1) for k in order], 1
    )
    basis_turn = jnp.concatenate(
        [lax.dynamic_slice_in_dim(by_column, k * half_in, half_in, 0) for k in (z_lo, 1 - z_lo)], 0
    )
    basis_rows = lax.dynamic_slice_in_dim(by_column, q * quarter, quarter, 0)

    cuts = [0, width // 4, width // 2, width]

    def rotated_out(k):
        lo, hi = cuts[k], cuts[k + 1]
        b = lo // block
        return dot(
            out_grads[:, b * block : (b + 1) * block], basis_out[b][:, lo - b * block : hi - b * block]
        ).astype(jnp.bfloat16)

    own_out = [rotated_out(k) for k in range(3)]

    other = swap_z_lo(mine)
    mine_parts = [mine, along_y(mine, -1), along_y(mine, 2), along_y(mine, 1)]
    other_parts = [other, along_y(other, -1), swap_z_lo(mine_parts[2]), along_y(other, 1)]

    gathered_out = []
    gate = mine
    for k in range(3):
        own = after(own_out[k], gate)
        parts = [own, along_x(own, -1), along_x(own, 2), along_x(own, 1)]
        together = jnp.concatenate(parts, 0)
        gate = together
        gathered_out.append((together, swap_core(together)))

    own_in = jnp.zeros((block // 2, 4 * tokens), jnp.bfloat16)
    send_in = jnp.zeros((block // 2, 4 * tokens), jnp.bfloat16)
    for d in (0, 1, 3, 2):
        part = jnp.concatenate([mine_parts[d], other_parts[d]], 1)
        turned = dot(basis_turn, part, ((0,), (1,))).astype(jnp.bfloat16)
        place = (y + d - x) % 4 * tokens
        own_in = lax.dynamic_update_slice_in_dim(own_in, turned[: block // 2], place, 1)
        send_in = lax.dynamic_update_slice_in_dim(send_in, turned[block // 2 :], place, 1)
    far_in = swap_core(send_in)
    own_in_sq = squared(own_in)
    far_in_sq = squared(far_in)

    pieces = []
    for k in range(3):
        near, far = gathered_out[k]
        step = width // 4
        for lo in range(0, near.shape[1], step):
            n, f = near[:, lo : lo + step], far[:, lo : lo + step]
            scale_part = dot(own_in_sq, squared(n)) + dot(far_in_sq, squared(f))
            grad_part = dot(own_in, n) + dot(far_in, f)
            send = jnp.stack([scale_part[quarter:], grad_part[quarter:]]).astype(jnp.bfloat16)
            got = swap_z_hi(send).astype(jnp.float32)
            scales = (scale_part[:quarter] + got[0]) / tokens_all
            grad = grad_part[:quarter] + got[1]
            rotated = (grad / math.sqrt(tokens_all) / (scales + damping)).astype(jnp.bfloat16)
            pieces.append((scales, rotated))

    naturals = []
    for b in range(width // block):
        rotated = jnp.concatenate([pieces[2 * b][1], pieces[2 * b + 1][1]], 1)
        half = dot(rotated, basis_out[b], ((1,), (1,))).astype(jnp.bfloat16)
        pair = jnp.concatenate([half, swap_z_hi(half)], 0)
        far_pair = swap_core(pair)
        naturals.append(
            (dot(basis_rows[:, : block // 2], pair) + dot(basis_rows[:, block // 2 :], far_pair)).astype(
                jnp.bfloat16
            )
        )
    scales = jnp.concatenate([s for s, _ in pieces], 1)
    natural = jnp.concatenate(naturals, 1)
    return (scales, natural)


def solution(mesh):
    return jax.shard_map(
        shards,
        mesh=mesh,
        in_specs=(P("dp", "tensor"), P("dp", "tensor"), P(), P("tensor", None, None)),
        out_specs=(P("dp", "tensor"), P("dp", "tensor")),
        check_vma=False,
    )
```

```python
import math

import jax
import jax.numpy as jnp
from jax import lax
from jax.experimental import pallas as pl
from jax.experimental.pallas import tpu as pltpu
from jax.sharding import Mesh
from jax.sharding import PartitionSpec as P

damping = 0.1


def along_y(v, d):
    return lax.ppermute(v, "y", [(i, (i + d) % 4) for i in range(4)])


def swap(v, axis):
    return lax.ppermute(v, axis, [(0, 1), (1, 0)])


def transpose_xy(v):
    return lax.ppermute(v, ("x", "y"), [(x * 4 + y, y * 4 + x) for x in range(4) for y in range(4)])


def squared(values):
    return values * values


def dot(left, right, contract=((1,), (0,))):
    return lax.dot_general(left, right, (contract, ((), ())), preferred_element_type=jnp.float32)


def fence(*values):
    return lax.optimization_barrier(values)


brief = pl.CostEstimate(flops=1, bytes_accessed=1, transcendentals=0)


def limit(mib):
    return pltpu.CompilerParams(vmem_limit_bytes=mib * 1024 * 1024)


def rotate_kernel(basis, first, second, out):
    tokens = first.shape[0]
    ways = ((1,), (1,))
    out[:, :tokens] = dot(basis[...], first[...], ways).astype(out.dtype)
    out[:, tokens:] = dot(basis[...], second[...], ways).astype(out.dtype)


def rotated(basis, first, second, side):
    tokens, depth = first.shape
    near = basis.shape[0] // 2
    tile = near // 2
    whole = pl.BlockSpec((tokens, depth), lambda i: (0, 0))
    return pl.pallas_call(
        rotate_kernel,
        grid=(2,),
        in_specs=[pl.BlockSpec((tile, depth), lambda i: (2 * side + i, 0)), whole, whole],
        out_specs=pl.BlockSpec((tile, 2 * tokens), lambda i: (i, 0)),
        out_shape=jax.ShapeDtypeStruct((near, 2 * tokens), jnp.bfloat16),
        compiler_params=limit(24),
        cost_estimate=brief,
        name="rotate_in",
    )(basis, first, second)


def contract_kernel(place, l0, l1, l2, l3, gathered, kept, send, left, left_sq, right, right_sq):
    depth = l0.shape[1]
    tokens = depth // 2
    quarter = kept.shape[1]

    @pl.when(pl.program_id(0) == 0)
    def _():
        for k, part in enumerate((l0, l1, l2, l3)):
            left[:, k * depth : (k + 1) * depth] = part[...]
            left_sq[:, k * depth : (k + 1) * depth] = squared(part[...])

    for k, (d, far) in enumerate(((0, 0), (2, 0), (0, 1), (2, 1), (1, 0), (3, 0), (1, 1), (3, 1))):
        index = (place[0] + d) % 4 * 2 + (place[1] + far) % 2
        part = gathered[pl.ds(pl.multiple_of(index * tokens, tokens), tokens), :]
        right[pl.ds(k * tokens, tokens), :] = part
        right_sq[pl.ds(k * tokens, tokens), :] = squared(part)

    scale_part = dot(left_sq[...], right_sq[...])
    grad_part = dot(left[...], right[...])
    kept[0] = scale_part[:quarter]
    kept[1] = grad_part[:quarter]
    send[0] = scale_part[quarter:].astype(send.dtype)
    send[1] = grad_part[quarter:].astype(send.dtype)


def contracted(place, lefts, gathered, lo, hi):
    near, depth = lefts[0].shape
    total = gathered.shape[0]
    tile = total // 12
    quarter = near // 2
    out_spec = pl.BlockSpec((2, quarter, tile), lambda i, s: (0, 0, i))
    return pl.pallas_call(
        contract_kernel,
        grid_spec=pltpu.PrefetchScalarGridSpec(
            num_scalar_prefetch=1,
            grid=((hi - lo) // tile,),
            in_specs=[pl.BlockSpec((near, depth), lambda i, s: (0, 0))] * 4
            + [pl.BlockSpec((total, tile), lambda i, s: (0, lo // tile + i))],
            out_specs=[out_spec, out_spec],
            scratch_shapes=[pltpu.VMEM((near, total), jnp.bfloat16)] * 2
            + [pltpu.VMEM((total, tile), jnp.bfloat16)] * 2,
        ),
        out_shape=[
            jax.ShapeDtypeStruct((2, quarter, hi - lo), jnp.float32),
            jax.ShapeDtypeStruct((2, quarter, hi - lo), jnp.bfloat16),
        ],
        compiler_params=limit(53),
        cost_estimate=brief,
        name="contract",
    )(place, *lefts, gathered)


def natural_kernel(left, basis, *refs):
    natural = refs[-1]
    natural[...] = dot(left[...], basis[...], ((1,), (1,))).astype(natural.dtype)


def natural_of(left, basis, natural, b, width):
    quarter, block = left.shape
    tile = 512
    held = [] if natural is None else [natural]
    return pl.pallas_call(
        natural_kernel,
        grid=(block // tile,),
        in_specs=[
            pl.BlockSpec((quarter, block), lambda i: (0, 0)),
            pl.BlockSpec((tile, block), lambda i: (i, 0)),
        ]
        + [pl.BlockSpec(memory_space=pl.ANY)] * len(held),
        out_specs=pl.BlockSpec((quarter, tile), lambda i: (0, b * block // tile + i)),
        out_shape=jax.ShapeDtypeStruct((quarter, width), jnp.bfloat16),
        input_output_aliases={2: 0} if held else {},
        compiler_params=pltpu.CompilerParams(vmem_limit_bytes=24 * 1024 * 1024),
        cost_estimate=brief,
        name="natural",
    )(left, basis, *held)


def shards(activations, out_grads, basis_in, basis_out):
    tokens, half_in = activations.shape
    block = basis_in.shape[1]
    width = out_grads.shape[1]
    quarter = block // 4
    near = block // 2
    x = lax.axis_index("x")
    y = lax.axis_index("y")
    z_lo = lax.axis_index("z_lo")
    core = lax.axis_index("core")
    q = 2 * lax.axis_index("z_hi") + core
    place = jnp.stack([y, core])

    mine = transpose_xy(activations)
    block_basis = lax.dynamic_index_in_dim(basis_in, x, 0, keepdims=False)
    order = [q, q ^ 2, q ^ 1, q ^ 3]
    by_column = jnp.concatenate(
        [lax.dynamic_slice_in_dim(block_basis, k * quarter, quarter, 1) for k in order], 1
    )
    basis_turn = jnp.concatenate(
        [lax.dynamic_slice_in_dim(by_column, k * half_in, half_in, 0) for k in (z_lo, 1 - z_lo)], 0
    ).T
    basis_rows = lax.dynamic_slice_in_dim(by_column, q * quarter, quarter, 0)

    def rotated_out(lo, hi):
        b = lo // block
        return dot(
            out_grads[:, b * block : (b + 1) * block], basis_out[b, :, lo - b * block : hi - b * block]
        ).astype(jnp.bfloat16)

    cut = block * 3 // 2
    first_out = jnp.concatenate([rotated_out(0, block), rotated_out(block, cut)], 1)
    second_out = rotated_out(cut, width)
    mine, basis_turn, basis_rows, second_out = fence(mine, basis_turn, basis_rows, second_out)
    gathered = [lax.all_gather(v, ("x", "core"), axis=0, tiled=True) for v in (first_out, second_out)]

    other = swap(mine, "z_lo")
    two = along_y(mine, 2)
    mine, other, two = fence(mine, other, two)

    whole = jnp.concatenate([mine, other], 1)
    below, above = along_y(whole, 1), along_y(whole, -1)
    two = jnp.concatenate([two, swap(two, "z_lo")], 1)
    send_in = rotated(basis_turn, whole, two, 1)
    early = [rotated(basis_turn, whole, two, 0), swap(send_in, "core")]
    below, above, *early = fence(below, above, *early)

    send_in = rotated(basis_turn, above, below, 1)
    lefts = early + [rotated(basis_turn, above, below, 0), swap(send_in, "core")]

    def finished(own, got):
        total = own + got.astype(jnp.float32)
        tokens_all = tokens * 16
        scales = total[0] / tokens_all
        turned = (total[1] / math.sqrt(tokens_all) / (scales + damping)).astype(jnp.bfloat16)
        return scales, turned

    def from_all_rows(turned, over):
        pair = jnp.concatenate([turned, over], 0)
        total = dot(basis_rows[:, :near], pair) + dot(basis_rows[:, near:], swap(pair, "core"))
        return total.astype(jnp.bfloat16)

    cuts = [0, block // 4, block // 2, block, block * 3 // 2, 2 * block]
    own, out = [], []
    for lo, hi in zip(cuts[:-1], cuts[1:]):
        piece = 0 if hi <= cut else 1
        here = gathered[piece]
        if out:
            here = fence(here, out[-1])[0]
        kept, send = contracted(place, lefts, here, lo - piece * cut, hi - piece * cut)
        own.append(kept)
        out.append(send)
    done = [finished(own[k], swap(out[k], "z_hi")) for k in range(5)]
    turned0 = jnp.concatenate([columns for _, columns in done[:3]], 1)
    left0 = from_all_rows(turned0, swap(turned0, "z_hi"))
    natural = natural_of(left0, basis_out[0], None, 0, width)
    left3 = from_all_rows(done[3][1], swap(done[3][1], "z_hi"))
    scales = jnp.concatenate([scale for scale, _ in done], 1)
    over4, left3, natural, scales = fence(swap(done[4][1], "z_hi"), left3, natural, scales)
    left4 = from_all_rows(done[4][1], over4)
    natural = natural_of(jnp.concatenate([left3, left4], 1), basis_out[1], natural, 1, width)
    return scales, natural


def solution(mesh):
    split = Mesh(mesh.devices.reshape(4, 2, 2, 4, 2), ("x", "z_hi", "core", "y", "z_lo"))
    dp, tensor = ("x", "z_hi", "core"), ("y", "z_lo")
    return jax.shard_map(
        shards,
        mesh=split,
        in_specs=(P(dp, tensor), P(dp, tensor), P(), P(tensor, None, None)),
        out_specs=(P(dp, tensor), P(dp, tensor)),
        check_vma=False,
    )
```

```python
import math

import jax
import jax.numpy as jnp
from jax import lax
from jax.experimental import pallas as pl
from jax.experimental.pallas import tpu as pltpu
from jax.sharding import Mesh
from jax.sharding import PartitionSpec as P

damping = 0.1


def along_y(v, d):
    return lax.ppermute(v, "y", [(i, (i + d) % 4) for i in range(4)])


def along_x(v, d):
    return lax.ppermute(v, "x", [(i, (i + d) % 4) for i in range(4)])


def swap(v, axis):
    return lax.ppermute(v, axis, [(0, 1), (1, 0)])


def transpose_xy(v):
    return lax.ppermute(v, ("x", "y"), [(x * 4 + y, y * 4 + x) for x in range(4) for y in range(4)])


def squared(values):
    return values * values


def dot(left, right, contract=((1,), (0,))):
    return lax.dot_general(left, right, (contract, ((), ())), preferred_element_type=jnp.float32)


def fence(*values):
    return lax.optimization_barrier(values)


brief = pl.CostEstimate(flops=1, bytes_accessed=1, transcendentals=0)


def limit(mib):
    return pltpu.CompilerParams(vmem_limit_bytes=mib * 1024 * 1024)


def pick_kernel(place, values, out):
    out[...] = values[...]


def partner_columns(place, values, block):
    rows = values.shape[0]
    return pl.pallas_call(
        pick_kernel,
        grid_spec=pltpu.PrefetchScalarGridSpec(
            num_scalar_prefetch=1,
            grid=(2,),
            in_specs=[pl.BlockSpec((rows, block // 2), lambda i, s: (0, (1 - s[0]) * 2 + i))],
            out_specs=pl.BlockSpec((rows, block // 2), lambda i, s: (0, i)),
        ),
        out_shape=jax.ShapeDtypeStruct((rows, block), values.dtype),
        compiler_params=limit(60),
        cost_estimate=brief,
        name="partner_columns",
    )(place, values)


def rotate_out_kernel(place, own, other, basis, *outs):
    tokens = own.shape[0]
    for k, out in enumerate(outs):

        @pl.when(pl.program_id(0) == k)
        def _(out=out):
            out[:tokens] = dot(own[...], basis[0]).astype(out.dtype)
            out[tokens:] = dot(other[...], basis[0]).astype(out.dtype)


def rotated_out(place, grads, other, basis):
    tokens, block = other.shape
    tile = block // 4
    shape = jax.ShapeDtypeStruct((2 * tokens, tile), jnp.bfloat16)
    return pl.pallas_call(
        rotate_out_kernel,
        grid_spec=pltpu.PrefetchScalarGridSpec(
            num_scalar_prefetch=1,
            grid=(4,),
            in_specs=[
                pl.BlockSpec((tokens, block), lambda i, s: (0, s[0])),
                pl.BlockSpec((tokens, block), lambda i, s: (0, 0)),
                pl.BlockSpec((1, block, tile), lambda i, s: (s[0], 0, i)),
            ],
            out_specs=[pl.BlockSpec(shape.shape, lambda i, s: (0, 0))] * 4,
        ),
        out_shape=[shape] * 4,
        compiler_params=limit(48),
        cost_estimate=brief,
        name="rotate_out",
    )(place, grads, other, basis)


def payload_kernel(below, above, *refs):
    *own, right, left = refs
    start = 0
    for values in own:
        start = values.shape[1]
        right[:, :start] = values[...]
        left[:, :start] = values[...]
    right[:, start:] = below[...]
    left[:, start:] = above[...]


def payloads(own, columns, below, above, mib=24):
    own = [] if own is None else [own]
    rows = below.shape[0]
    half = columns // 2
    shape = jax.ShapeDtypeStruct((rows, sum(v.shape[1] for v in own) + half), jnp.bfloat16)
    whole = pl.BlockSpec(shape.shape, lambda i: (0, 0))
    return pl.pallas_call(
        payload_kernel,
        grid=(1,),
        in_specs=[pl.BlockSpec((rows, half), lambda i: (0, 0)), pl.BlockSpec((rows, half), lambda i: (0, 1))]
        + [pl.BlockSpec(v.shape, lambda i: (0, 0)) for v in own],
        out_specs=[whole, whole],
        out_shape=[shape, shape],
        compiler_params=limit(mib),
        cost_estimate=brief,
        name="payload",
    )(below, above, *own)


def rotate_kernel(basis, first, second, out):
    tokens = first.shape[0]
    ways = ((1,), (1,))
    out[:, :tokens] = dot(basis[...], first[...], ways).astype(out.dtype)
    out[:, tokens:] = dot(basis[...], second[...], ways).astype(out.dtype)


def rotated(basis, first, second):
    tokens, depth = first.shape
    features = basis.shape[0]
    tile = features // 4
    whole = pl.BlockSpec((tokens, depth), lambda i: (0, 0))
    return pl.pallas_call(
        rotate_kernel,
        grid=(4,),
        in_specs=[pl.BlockSpec((tile, depth), lambda i: (i, 0)), whole, whole],
        out_specs=pl.BlockSpec((tile, 2 * tokens), lambda i: (i, 0)),
        out_shape=jax.ShapeDtypeStruct((features, 2 * tokens), jnp.bfloat16),
        compiler_params=limit(24),
        cost_estimate=brief,
        name="rotate_in",
    )(basis, first, second)


def contract_kernel(place, early, early_far, late, late_far, own, above, below, right, left, *refs):
    kept, send, features, grads, feature_sems, grad_sems = refs
    tokens = features.shape[2] // 2
    columns = grads.shape[2]
    half = columns // 2
    rows = kept.shape[1]

    def feature_copies(e, index, sources):
        for far, source in enumerate(sources):
            start = pl.multiple_of(index // 2 * tokens, tokens)
            yield pltpu.make_async_copy(
                source.at[:, pl.ds(start, tokens)],
                features.at[e, :, pl.ds(far * tokens, tokens)],
                feature_sems.at[e, far],
            )

    def grad_copies(e):
        if e == 2:
            start = right.shape[1] - half
            pairs = [(right.at[:, pl.ds(start, half)], 0), (left.at[:, pl.ds(start, half)], half)]
        else:
            source = {0: own, 1: above, 3: below}[e]
            pairs = [(source.at[:, pl.ds(k * half, half)], k * half) for k in range(2)]
        for k, (source, start) in enumerate(pairs):
            yield pltpu.make_async_copy(source, grads.at[e, :, pl.ds(start, half)], grad_sems.at[e, k])

    for e in range(4):
        index = (place[0] + e) % 4
        for copy in grad_copies(e):
            copy.start()
        for odd, sources in enumerate(((early, early_far), (late, late_far))):

            @pl.when(index % 2 == odd)
            def _(e=e, index=index, sources=sources):
                for copy in feature_copies(e, index, sources):
                    copy.start()

    scale_part, grad_part = None, None
    for e in range(4):
        for copy in grad_copies(e):
            copy.wait()
        for copy in feature_copies(e, 0, (early, early_far)):
            copy.wait()
        part, values = features[e], grads[e]
        grad = dot(part, values)
        scale = dot(squared(part), squared(values))
        grad_part = grad if e == 0 else grad_part + grad
        scale_part = scale if e == 0 else scale_part + scale
    kept[0] = scale_part[:rows]
    kept[1] = grad_part[:rows]
    send[0] = scale_part[rows:].astype(send.dtype)
    send[1] = grad_part[rows:].astype(send.dtype)


def contracted(place, lefts, own, brought, following):
    features, depth = lefts[0].shape
    tokens, columns = own.shape
    rows = features // 2
    out_spec = pl.BlockSpec((2, rows, columns), lambda i, s: (0, 0, 0))
    return pl.pallas_call(
        contract_kernel,
        grid_spec=pltpu.PrefetchScalarGridSpec(
            num_scalar_prefetch=1,
            grid=(1,),
            in_specs=[pl.BlockSpec(memory_space=pl.ANY)] * 9,
            out_specs=[out_spec, out_spec],
            scratch_shapes=[
                pltpu.VMEM((4, features, depth), jnp.bfloat16),
                pltpu.VMEM((4, tokens, columns), jnp.bfloat16),
                pltpu.SemaphoreType.DMA((4, 2)),
                pltpu.SemaphoreType.DMA((4, 2)),
            ],
        ),
        out_shape=[
            jax.ShapeDtypeStruct((2, rows, columns), jnp.float32),
            jax.ShapeDtypeStruct((2, rows, columns), jnp.bfloat16),
        ],
        compiler_params=limit(56),
        cost_estimate=brief,
        name="contract",
    )(place, *lefts, own, brought[1], brought[0], *following)


def natural_kernel(place, left, basis, natural):
    natural[...] = dot(left[...], basis[0], ((1,), (1,))).astype(natural.dtype)


def natural_rows(place, left, basis, whose):
    rows, block = left.shape
    tile = block // 2
    return pl.pallas_call(
        natural_kernel,
        grid_spec=pltpu.PrefetchScalarGridSpec(
            num_scalar_prefetch=1,
            grid=(2,),
            in_specs=[
                pl.BlockSpec((rows // 2, block), lambda i, s: (s[0] ^ whose, 0)),
                pl.BlockSpec((1, tile, block), lambda i, s: (s[0], i, 0)),
            ],
            out_specs=pl.BlockSpec((rows // 2, tile), lambda i, s: (0, i)),
        ),
        out_shape=jax.ShapeDtypeStruct((rows // 2, block), jnp.bfloat16),
        compiler_params=limit(24),
        cost_estimate=brief,
        name="natural",
    )(place, left, basis)


def place_kernel(place, own, other, out):
    @pl.when(pl.program_id(0) == place[0])
    def _():
        out[...] = own[...]

    @pl.when(pl.program_id(0) != place[0])
    def _():
        out[...] = other[...]


def side_by_side(place, own, other):
    rows, block = own.shape
    whole = pl.BlockSpec((rows, block), lambda i, s: (0, 0))
    return pl.pallas_call(
        place_kernel,
        grid_spec=pltpu.PrefetchScalarGridSpec(
            num_scalar_prefetch=1,
            grid=(2,),
            in_specs=[whole, whole],
            out_specs=pl.BlockSpec((rows, block), lambda i, s: (0, i)),
        ),
        out_shape=jax.ShapeDtypeStruct((rows, 2 * block), own.dtype),
        compiler_params=limit(24),
        cost_estimate=brief,
        name="side_by_side",
    )(place, own, other)


def shards(activations, out_grads, basis_in, basis_out):
    tokens, half_in = activations.shape
    block = basis_in.shape[1]
    near = block // 2
    x = lax.axis_index("x")
    y = lax.axis_index("y")
    z_lo = lax.axis_index("z_lo")
    z_hi = lax.axis_index("z_hi")
    core = lax.axis_index("core")
    turn = jnp.reshape((x - y) % 4, (1,))
    place = jnp.reshape(core, (1,))

    mine = transpose_xy(activations)
    other_out = swap(partner_columns(place, out_grads, block), "core")
    block_basis = lax.dynamic_index_in_dim(basis_in, x, 0, keepdims=False)
    by_column = jnp.concatenate(
        [lax.dynamic_slice_in_dim(block_basis, k * near, near, 1) for k in (z_hi, 1 - z_hi)], 1
    )
    basis_turn = jnp.concatenate(
        [lax.dynamic_slice_in_dim(by_column, k * half_in, half_in, 0) for k in (z_lo, 1 - z_lo)], 0
    ).T
    basis_rows = lax.dynamic_slice_in_dim(by_column, z_hi * near, near, 0)
    own_out = rotated_out(place, out_grads, other_out, basis_out)

    def around_x(right, left):
        return [along_x(right, 1), along_x(left, -1)]

    mine, basis_turn, basis_rows, *own_out = fence(mine, basis_turn, basis_rows, *own_out)
    columns = own_out[0].shape[1]

    other = swap(mine, "z_lo")
    two = along_y(mine, 2)
    first = around_x(own_out[0], own_out[0])
    mine, other, two, *first = fence(mine, other, two, *first)

    whole = jnp.concatenate([mine, other], 1)
    sent = payloads(own_out[1], columns, *first)
    whole, two, *sent = fence(whole, two, *sent)
    below, above = along_y(whole, 1), along_y(whole, -1)
    second = around_x(*sent)
    two = jnp.concatenate([two, swap(two, "z_lo")], 1)
    early = rotated(basis_turn, whole, two)
    below, above, early, *second = fence(below, above, early, *second)

    def finished(kept, got):
        total = kept + got.astype(jnp.float32)
        tokens_all = tokens * 16
        scales = total[0] / tokens_all
        turned = (total[1] / math.sqrt(tokens_all) / (scales + damping)).astype(jnp.bfloat16)
        return scales, turned

    def product(turned, over):
        total = dot(basis_rows[:, :near], turned) + dot(basis_rows[:, near:], over)
        return total.astype(jnp.bfloat16)

    third = around_x(*payloads(own_out[2], columns, *second))
    late = rotated(basis_turn, above, below)
    lefts = [early, swap(early, "core"), late, swap(late, "core")]
    kept0, send0 = contracted(turn, lefts, own_out[0], first, second)
    got0 = swap(send0, "z_hi")
    *third, send0 = fence(*third, send0)
    fourth = around_x(*payloads(own_out[3], columns, *third))
    own1, got0 = fence(own_out[1], got0)
    kept1, send1 = contracted(turn, lefts, own1, second, third)
    got1 = swap(send1, "z_hi")
    scales0, turned0 = finished(kept0, got0)
    *fourth, send1, over0 = fence(*fourth, send1, swap(turned0, "z_hi"))
    fifth = around_x(*payloads(None, columns, *fourth, mib=60))
    kept2, send2 = contracted(turn, lefts, own_out[2], third, fourth)
    got2 = swap(send2, "z_hi")
    *fifth, send2, got1 = fence(*fifth, send2, got1)
    kept3, send3 = contracted(turn, lefts, own_out[3], fourth, fifth)

    got3 = swap(send3, "z_hi")
    got1, _ = fence(got1, send3)
    done = [(scales0, turned0)] + [finished(*pair) for pair in ((kept1, got1), (kept2, got2), (kept3, got3))]
    left01 = product(turned0, over0)
    left12 = product(done[1][1], swap(done[1][1], "z_hi"))
    left2 = product(done[2][1], swap(done[2][1], "z_hi"))
    over3 = swap(done[3][1], "z_hi")
    scales = jnp.concatenate([scale for scale, _ in done], 1)
    quarter = near // 2
    scales_own = lax.dynamic_slice_in_dim(scales, core * quarter, quarter, 0)
    scales_other = swap(lax.dynamic_slice_in_dim(scales, (1 - core) * quarter, quarter, 0), "core")
    scales = side_by_side(place, scales_own, scales_other)
    over3, left2, left12, left01, scales = fence(over3, left2, left12, left01, scales)
    left = jnp.concatenate([left01, left12, left2, product(done[3][1], over3)], 1)
    natural_other = swap(natural_rows(place, left, basis_out, 1), "core")
    natural = side_by_side(place, natural_rows(place, left, basis_out, 0), natural_other)
    return scales, natural


def solution(mesh):
    split = Mesh(mesh.devices.reshape(4, 2, 2, 4, 2), ("x", "z_hi", "core", "y", "z_lo"))
    dp, tensor = ("x", "z_hi", "core"), ("y", "z_lo")
    return jax.shard_map(
        shards,
        mesh=split,
        in_specs=(P(dp, tensor), P(dp, tensor), P(), P(tensor, None, None)),
        out_specs=(P(dp, tensor), P(dp, tensor)),
        check_vma=False,
    )
```

```python
import functools
import math

import jax
import jax.numpy as jnp
from jax import lax
from jax.experimental import pallas as pl
from jax.experimental.pallas import tpu as pltpu
from jax.sharding import Mesh
from jax.sharding import PartitionSpec as P

damping = 0.1


def along_y(v, d):
    return lax.ppermute(v, "y", [(i, (i + d) % 4) for i in range(4)])


def along_x(v, d):
    return lax.ppermute(v, "x", [(i, (i + d) % 4) for i in range(4)])


def swap(v, axis):
    return lax.ppermute(v, axis, [(0, 1), (1, 0)])


def transpose_xy(v):
    return lax.ppermute(v, ("x", "y"), [(x * 4 + y, y * 4 + x) for x in range(4) for y in range(4)])


def squared(values):
    return values * values


def dot(left, right, contract=((1,), (0,))):
    return lax.dot_general(left, right, (contract, ((), ())), preferred_element_type=jnp.float32)


def fence(*values):
    return lax.optimization_barrier(values)


brief = pl.CostEstimate(flops=1, bytes_accessed=1, transcendentals=0)


def limit(mib):
    return pltpu.CompilerParams(vmem_limit_bytes=mib * 1024 * 1024)


def pick_kernel(place, values, out):
    out[...] = values[...]


def partner_columns(place, values, block):
    rows = values.shape[0]
    return pl.pallas_call(
        pick_kernel,
        grid_spec=pltpu.PrefetchScalarGridSpec(
            num_scalar_prefetch=1,
            grid=(2,),
            in_specs=[pl.BlockSpec((rows, block // 2), lambda i, s: (0, (1 - s[0]) * 2 + i))],
            out_specs=pl.BlockSpec((rows, block // 2), lambda i, s: (0, i)),
        ),
        out_shape=jax.ShapeDtypeStruct((rows, block), values.dtype),
        compiler_params=limit(60),
        cost_estimate=brief,
        name="partner_columns",
    )(place, values)


def rotate_out_kernel(place, own, other, basis, *outs):
    tokens = own.shape[0]
    for k, out in enumerate(outs):

        @pl.when(pl.program_id(0) == k)
        def _(out=out):
            out[:tokens] = dot(own[...], basis[0]).astype(out.dtype)
            out[tokens:] = dot(other[...], basis[0]).astype(out.dtype)


def rotated_out(place, grads, other, basis):
    tokens, block = other.shape
    tile = block // 4
    shape = jax.ShapeDtypeStruct((2 * tokens, tile), jnp.bfloat16)
    return pl.pallas_call(
        rotate_out_kernel,
        grid_spec=pltpu.PrefetchScalarGridSpec(
            num_scalar_prefetch=1,
            grid=(4,),
            in_specs=[
                pl.BlockSpec((tokens, block), lambda i, s: (0, s[0])),
                pl.BlockSpec((tokens, block), lambda i, s: (0, 0)),
                pl.BlockSpec((1, block, tile), lambda i, s: (s[0], 0, i)),
            ],
            out_specs=[pl.BlockSpec(shape.shape, lambda i, s: (0, 0))] * 4,
        ),
        out_shape=[shape] * 4,
        compiler_params=limit(48),
        cost_estimate=brief,
        name="rotate_out",
    )(place, grads, other, basis)


def payload_kernel(below, above, *refs):
    *own, right, left = refs
    start = 0
    for values in own:
        start = values.shape[1]
        right[:, :start] = values[...]
        left[:, :start] = values[...]
    right[:, start:] = below[...]
    left[:, start:] = above[...]


def payloads(own, columns, below, above, mib=24):
    own = [] if own is None else [own]
    rows = below.shape[0]
    half = columns // 2
    shape = jax.ShapeDtypeStruct((rows, sum(v.shape[1] for v in own) + half), jnp.bfloat16)
    whole = pl.BlockSpec(shape.shape, lambda i: (0, 0))
    return pl.pallas_call(
        payload_kernel,
        grid=(1,),
        in_specs=[pl.BlockSpec((rows, half), lambda i: (0, 0)), pl.BlockSpec((rows, half), lambda i: (0, 1))]
        + [pl.BlockSpec(v.shape, lambda i: (0, 0)) for v in own],
        out_specs=[whole, whole],
        out_shape=[shape, shape],
        compiler_params=limit(mib),
        cost_estimate=brief,
        name="payload",
    )(below, above, *own)


def rotate_kernel(basis, first, second, out):
    tokens = first.shape[0]
    ways = ((1,), (1,))
    out[:, :tokens] = dot(basis[...], first[...], ways).astype(out.dtype)
    out[:, tokens:] = dot(basis[...], second[...], ways).astype(out.dtype)


def rotated(basis, first, second):
    tokens, depth = first.shape
    features = basis.shape[0]
    tile = features // 4
    whole = pl.BlockSpec((tokens, depth), lambda i: (0, 0))
    return pl.pallas_call(
        rotate_kernel,
        grid=(4,),
        in_specs=[pl.BlockSpec((tile, depth), lambda i: (i, 0)), whole, whole],
        out_specs=pl.BlockSpec((tile, 2 * tokens), lambda i: (i, 0)),
        out_shape=jax.ShapeDtypeStruct((features, 2 * tokens), jnp.bfloat16),
        compiler_params=limit(24),
        cost_estimate=brief,
        name="rotate_in",
    )(basis, first, second)


def contract_kernel(part, place, early, early_far, late, late_far, own, above, below, right, left, *refs):
    kept, send, features, grads, feature_sems, grad_sems = refs
    tokens = features.shape[2] // 2
    half = own.shape[1] // 2
    rows = kept.shape[1]
    halves = range(2) if part is None else (part,)

    def feature_copies(e, index, sources):
        for far, source in enumerate(sources):
            start = pl.multiple_of(index // 2 * tokens, tokens)
            yield pltpu.make_async_copy(
                source.at[:, pl.ds(start, tokens)],
                features.at[e, :, pl.ds(far * tokens, tokens)],
                feature_sems.at[e, far],
            )

    def grad_copies(e):
        for slot, k in enumerate(halves):
            if e == 2:
                source = (right, left)[k]
                start = source.shape[1] - half
            else:
                source = {0: own, 1: above, 3: below}[e]
                start = k * half
            yield pltpu.make_async_copy(
                source.at[:, pl.ds(start, half)],
                grads.at[e, :, pl.ds(slot * half, half)],
                grad_sems.at[e, slot],
            )

    for e in range(4):
        index = (place[0] + e) % 4
        for copy in grad_copies(e):
            copy.start()
        for odd, sources in enumerate(((early, early_far), (late, late_far))):

            @pl.when(index % 2 == odd)
            def _(e=e, index=index, sources=sources):
                for copy in feature_copies(e, index, sources):
                    copy.start()

    scale_part, grad_part = None, None
    for e in range(4):
        for copy in grad_copies(e):
            copy.wait()
        for copy in feature_copies(e, 0, (early, early_far)):
            copy.wait()
        rotated_in, values = features[e], grads[e]
        grad = dot(rotated_in, values)
        scale = dot(squared(rotated_in), squared(values))
        grad_part = grad if e == 0 else grad_part + grad
        scale_part = scale if e == 0 else scale_part + scale
    kept[0] = scale_part[:rows]
    kept[1] = grad_part[:rows]
    send[0] = scale_part[rows:].astype(send.dtype)
    send[1] = grad_part[rows:].astype(send.dtype)


def contracted(place, lefts, own, brought, following, part=None):
    features, depth = lefts[0].shape
    tokens, columns = own.shape
    columns = columns if part is None else columns // 2
    rows = features // 2
    out_spec = pl.BlockSpec((2, rows, columns), lambda i, s: (0, 0, 0))
    return pl.pallas_call(
        functools.partial(contract_kernel, part),
        grid_spec=pltpu.PrefetchScalarGridSpec(
            num_scalar_prefetch=1,
            grid=(1,),
            in_specs=[pl.BlockSpec(memory_space=pl.ANY)] * 9,
            out_specs=[out_spec, out_spec],
            scratch_shapes=[
                pltpu.VMEM((4, features, depth), jnp.bfloat16),
                pltpu.VMEM((4, tokens, columns), jnp.bfloat16),
                pltpu.SemaphoreType.DMA((4, 2)),
                pltpu.SemaphoreType.DMA((4, 2)),
            ],
        ),
        out_shape=[
            jax.ShapeDtypeStruct((2, rows, columns), jnp.float32),
            jax.ShapeDtypeStruct((2, rows, columns), jnp.bfloat16),
        ],
        compiler_params=limit(56),
        cost_estimate=brief,
        name="contract",
    )(place, *lefts, own, brought[1], brought[0], *following)


def natural_kernel(place, left, basis, natural):
    natural[...] = dot(left[...], basis[0], ((1,), (1,))).astype(natural.dtype)


def natural_rows(place, left, basis, whose):
    rows, block = left.shape
    tile = block // 2
    return pl.pallas_call(
        natural_kernel,
        grid_spec=pltpu.PrefetchScalarGridSpec(
            num_scalar_prefetch=1,
            grid=(2,),
            in_specs=[
                pl.BlockSpec((rows // 2, block), lambda i, s: (s[0] ^ whose, 0)),
                pl.BlockSpec((1, tile, block), lambda i, s: (s[0], i, 0)),
            ],
            out_specs=pl.BlockSpec((rows // 2, tile), lambda i, s: (0, i)),
        ),
        out_shape=jax.ShapeDtypeStruct((rows // 2, block), jnp.bfloat16),
        compiler_params=limit(24),
        cost_estimate=brief,
        name="natural",
    )(place, left, basis)


def place_kernel(place, own, other, out):
    @pl.when(pl.program_id(0) == place[0])
    def _():
        out[...] = own[...]

    @pl.when(pl.program_id(0) != place[0])
    def _():
        out[...] = other[...]


def side_by_side(place, own, other):
    rows, block = own.shape
    whole = pl.BlockSpec((rows, block), lambda i, s: (0, 0))
    return pl.pallas_call(
        place_kernel,
        grid_spec=pltpu.PrefetchScalarGridSpec(
            num_scalar_prefetch=1,
            grid=(2,),
            in_specs=[whole, whole],
            out_specs=pl.BlockSpec((rows, block), lambda i, s: (0, i)),
        ),
        out_shape=jax.ShapeDtypeStruct((rows, 2 * block), own.dtype),
        compiler_params=limit(24),
        cost_estimate=brief,
        name="side_by_side",
    )(place, own, other)


def shards(activations, out_grads, basis_in, basis_out):
    tokens, half_in = activations.shape
    block = basis_in.shape[1]
    near = block // 2
    x = lax.axis_index("x")
    y = lax.axis_index("y")
    z_lo = lax.axis_index("z_lo")
    z_hi = lax.axis_index("z_hi")
    core = lax.axis_index("core")
    turn = jnp.reshape((x - y) % 4, (1,))
    place = jnp.reshape(core, (1,))

    mine = transpose_xy(activations)
    other_out = swap(partner_columns(place, out_grads, block), "core")
    block_basis = lax.dynamic_index_in_dim(basis_in, x, 0, keepdims=False)
    by_column = jnp.concatenate(
        [lax.dynamic_slice_in_dim(block_basis, k * near, near, 1) for k in (z_hi, 1 - z_hi)], 1
    )
    basis_turn = jnp.concatenate(
        [lax.dynamic_slice_in_dim(by_column, k * half_in, half_in, 0) for k in (z_lo, 1 - z_lo)], 0
    ).T
    basis_rows = lax.dynamic_slice_in_dim(by_column, z_hi * near, near, 0)
    own_out = rotated_out(place, out_grads, other_out, basis_out)

    def around_x(right, left):
        return [along_x(right, 1), along_x(left, -1)]

    mine, basis_turn, basis_rows, *own_out = fence(mine, basis_turn, basis_rows, *own_out)
    columns = own_out[0].shape[1]

    other = swap(mine, "z_lo")
    two = along_y(mine, 2)
    first = around_x(own_out[0], own_out[0])
    mine, other, two = fence(mine, other, two)

    whole = jnp.concatenate([mine, other], 1)
    below, above = along_y(whole, 1), along_y(whole, -1)
    second = around_x(*payloads(own_out[1], columns, *first))
    two = jnp.concatenate([two, swap(two, "z_lo")], 1)
    early = rotated(basis_turn, whole, two)
    below, above, early, *second = fence(below, above, early, *second)

    def finished(kept, got):
        total = kept + got.astype(jnp.float32)
        tokens_all = tokens * 16
        scales = total[0] / tokens_all
        turned = (total[1] / math.sqrt(tokens_all) / (scales + damping)).astype(jnp.bfloat16)
        return scales, turned

    def product(turned, over):
        total = dot(basis_rows[:, :near], turned) + dot(basis_rows[:, near:], over)
        return total.astype(jnp.bfloat16)

    third = around_x(*payloads(own_out[2], columns, *second))
    late = rotated(basis_turn, above, below)
    lefts = [early, swap(early, "core"), late, swap(late, "core")]
    kept0, send0 = contracted(turn, lefts, own_out[0], first, second, 0)
    own0, send0 = fence(own_out[0], send0)
    kept0b, send0b = contracted(turn, lefts, own0, first, second, 1)
    got0, got0b = swap(send0, "z_hi"), swap(send0b, "z_hi")
    *third, send0b = fence(*third, send0b)
    fourth = around_x(*payloads(own_out[3], columns, *third))
    own1, got0 = fence(own_out[1], got0)
    kept1, send1 = contracted(turn, lefts, own1, second, third)
    got1 = swap(send1, "z_hi")
    scales0, turned0 = finished(kept0, got0)
    scales0b, turned0b = finished(kept0b, got0b)
    scales0 = jnp.concatenate([scales0, scales0b], 1)
    turned0 = jnp.concatenate([turned0, turned0b], 1)
    over0 = swap(turned0, "z_hi")
    *fourth, send1 = fence(*fourth, send1)
    fifth = around_x(*payloads(None, columns, *fourth, mib=60))
    kept2, send2 = contracted(turn, lefts, own_out[2], third, fourth)
    got2 = swap(send2, "z_hi")
    *fifth, send2, got1, over0 = fence(*fifth, send2, got1, over0)
    kept3, send3 = contracted(turn, lefts, own_out[3], fourth, fifth)

    got3 = swap(send3, "z_hi")
    got1, _ = fence(got1, send3)
    done = [(scales0, turned0)] + [finished(*pair) for pair in ((kept1, got1), (kept2, got2), (kept3, got3))]
    left01 = product(turned0, over0)
    left12 = product(done[1][1], swap(done[1][1], "z_hi"))
    left2 = product(done[2][1], swap(done[2][1], "z_hi"))
    over3 = swap(done[3][1], "z_hi")
    scales = jnp.concatenate([scale for scale, _ in done], 1)
    quarter = near // 2
    scales_own = lax.dynamic_slice_in_dim(scales, core * quarter, quarter, 0)
    scales_other = swap(lax.dynamic_slice_in_dim(scales, (1 - core) * quarter, quarter, 0), "core")
    scales = side_by_side(place, scales_own, scales_other)
    over3, left2, left12, left01, scales = fence(over3, left2, left12, left01, scales)
    left = jnp.concatenate([left01, left12, left2, product(done[3][1], over3)], 1)
    natural_other = swap(natural_rows(place, left, basis_out, 1), "core")
    natural = side_by_side(place, natural_rows(place, left, basis_out, 0), natural_other)
    return scales, natural


def solution(mesh):
    split = Mesh(mesh.devices.reshape(4, 2, 2, 4, 2), ("x", "z_hi", "core", "y", "z_lo"))
    dp, tensor = ("x", "z_hi", "core"), ("y", "z_lo")
    return jax.shard_map(
        shards,
        mesh=split,
        in_specs=(P(dp, tensor), P(dp, tensor), P(), P(tensor, None, None)),
        out_specs=(P(dp, tensor), P(dp, tensor)),
        check_vma=False,
    )
```

```python
import functools
import math

import jax
import jax.numpy as jnp
from jax import lax
from jax.experimental import pallas as pl
from jax.experimental.pallas import tpu as pltpu
from jax.sharding import Mesh
from jax.sharding import PartitionSpec as P

damping = 0.1


def along_y(v, d):
    return lax.ppermute(v, "y", [(i, (i + d) % 4) for i in range(4)])


def along_x(v, d):
    return lax.ppermute(v, "x", [(i, (i + d) % 4) for i in range(4)])


def swap(v, axis):
    return lax.ppermute(v, axis, [(0, 1), (1, 0)])


def transpose_xy(v):
    return lax.ppermute(v, ("x", "y"), [(x * 4 + y, y * 4 + x) for x in range(4) for y in range(4)])


def squared(values):
    return values * values


def dot(left, right, contract=((1,), (0,))):
    return lax.dot_general(left, right, (contract, ((), ())), preferred_element_type=jnp.float32)


def fence(*values):
    return lax.optimization_barrier(values)


brief = pl.CostEstimate(flops=1, bytes_accessed=1, transcendentals=0)


def limit(mib):
    return pltpu.CompilerParams(vmem_limit_bytes=mib * 1024 * 1024)


def pick_kernel(place, values, out):
    out[...] = values[...]


def partner_columns(place, values, block):
    rows = values.shape[0]
    return pl.pallas_call(
        pick_kernel,
        grid_spec=pltpu.PrefetchScalarGridSpec(
            num_scalar_prefetch=1,
            grid=(2,),
            in_specs=[pl.BlockSpec((rows, block // 2), lambda i, s: (0, (1 - s[0]) * 2 + i))],
            out_specs=pl.BlockSpec((rows, block // 2), lambda i, s: (0, i)),
        ),
        out_shape=jax.ShapeDtypeStruct((rows, block), values.dtype),
        compiler_params=limit(60),
        cost_estimate=brief,
        name="partner_columns",
    )(place, values)


def rotate_out_kernel(place, own, other, basis, *outs):
    tokens = own.shape[0]
    for k, out in enumerate(outs):

        @pl.when(pl.program_id(0) == k)
        def _(out=out):
            out[:tokens] = dot(own[...], basis[0]).astype(out.dtype)
            out[tokens:] = dot(other[...], basis[0]).astype(out.dtype)


def rotated_out(place, grads, other, basis):
    tokens, block = other.shape
    tile = block // 4
    shape = jax.ShapeDtypeStruct((2 * tokens, tile), jnp.bfloat16)
    return pl.pallas_call(
        rotate_out_kernel,
        grid_spec=pltpu.PrefetchScalarGridSpec(
            num_scalar_prefetch=1,
            grid=(4,),
            in_specs=[
                pl.BlockSpec((tokens, block), lambda i, s: (0, s[0])),
                pl.BlockSpec((tokens, block), lambda i, s: (0, 0)),
                pl.BlockSpec((1, block, tile), lambda i, s: (s[0], 0, i)),
            ],
            out_specs=[pl.BlockSpec(shape.shape, lambda i, s: (0, 0))] * 4,
        ),
        out_shape=[shape] * 4,
        compiler_params=limit(48),
        cost_estimate=brief,
        name="rotate_out",
    )(place, grads, other, basis)


def payload_kernel(below, above, *refs):
    *own, right, left = refs
    start = 0
    for values in own:
        start = values.shape[1]
        right[:, :start] = values[...]
        left[:, :start] = values[...]
    right[:, start:] = below[...]
    left[:, start:] = above[...]


def payloads(own, columns, below, above, mib=24):
    own = [] if own is None else [own]
    rows = below.shape[0]
    half = columns // 2
    shape = jax.ShapeDtypeStruct((rows, sum(v.shape[1] for v in own) + half), jnp.bfloat16)
    whole = pl.BlockSpec(shape.shape, lambda i: (0, 0))
    return pl.pallas_call(
        payload_kernel,
        grid=(1,),
        in_specs=[pl.BlockSpec((rows, half), lambda i: (0, 0)), pl.BlockSpec((rows, half), lambda i: (0, 1))]
        + [pl.BlockSpec(v.shape, lambda i: (0, 0)) for v in own],
        out_specs=[whole, whole],
        out_shape=[shape, shape],
        compiler_params=limit(mib),
        cost_estimate=brief,
        name="payload",
    )(below, above, *own)


def rotate_kernel(basis, first, second, out):
    tokens = first.shape[0]
    ways = ((1,), (1,))
    out[:, :tokens] = dot(basis[...], first[...], ways).astype(out.dtype)
    out[:, tokens:] = dot(basis[...], second[...], ways).astype(out.dtype)


def rotated(basis, first, second):
    tokens, depth = first.shape
    features = basis.shape[0]
    tile = features // 4
    whole = pl.BlockSpec((tokens, depth), lambda i: (0, 0))
    return pl.pallas_call(
        rotate_kernel,
        grid=(4,),
        in_specs=[pl.BlockSpec((tile, depth), lambda i: (i, 0)), whole, whole],
        out_specs=pl.BlockSpec((tile, 2 * tokens), lambda i: (i, 0)),
        out_shape=jax.ShapeDtypeStruct((features, 2 * tokens), jnp.bfloat16),
        compiler_params=limit(24),
        cost_estimate=brief,
        name="rotate_in",
    )(basis, first, second)


def contract_kernel(part, place, early, early_far, late, late_far, own, above, below, right, left, *refs):
    kept, send, features, grads, feature_sems, grad_sems = refs
    tokens = features.shape[2] // 2
    half = own.shape[1] // 2
    rows = kept.shape[1]
    halves = range(2) if part is None else (part,)

    def feature_copies(e, index, sources):
        for far, source in enumerate(sources):
            start = pl.multiple_of(index // 2 * tokens, tokens)
            yield pltpu.make_async_copy(
                source.at[:, pl.ds(start, tokens)],
                features.at[e, :, pl.ds(far * tokens, tokens)],
                feature_sems.at[e, far],
            )

    def grad_copies(e):
        for slot, k in enumerate(halves):
            if e == 2:
                source = (right, left)[k]
                start = source.shape[1] - half
            else:
                source = {0: own, 1: above, 3: below}[e]
                start = k * half
            yield pltpu.make_async_copy(
                source.at[:, pl.ds(start, half)],
                grads.at[e, :, pl.ds(slot * half, half)],
                grad_sems.at[e, slot],
            )

    for e in range(4):
        index = (place[0] + e) % 4
        for copy in grad_copies(e):
            copy.start()
        for odd, sources in enumerate(((early, early_far), (late, late_far))):

            @pl.when(index % 2 == odd)
            def _(e=e, index=index, sources=sources):
                for copy in feature_copies(e, index, sources):
                    copy.start()

    scale_part, grad_part = None, None
    for e in range(4):
        for copy in grad_copies(e):
            copy.wait()
        for copy in feature_copies(e, 0, (early, early_far)):
            copy.wait()
        rotated_in, values = features[e], grads[e]
        grad = dot(rotated_in, values)
        scale = dot(squared(rotated_in), squared(values))
        grad_part = grad if e == 0 else grad_part + grad
        scale_part = scale if e == 0 else scale_part + scale
    kept[0] = scale_part[:rows]
    kept[1] = grad_part[:rows]
    send[0] = scale_part[rows:].astype(send.dtype)
    send[1] = grad_part[rows:].astype(send.dtype)


def contracted(place, lefts, own, brought, following, part=None, mib=32):
    features, depth = lefts[0].shape
    tokens, columns = own.shape
    columns = columns if part is None else columns // 2
    rows = features // 2
    out_spec = pl.BlockSpec((2, rows, columns), lambda i, s: (0, 0, 0))
    return pl.pallas_call(
        functools.partial(contract_kernel, part),
        grid_spec=pltpu.PrefetchScalarGridSpec(
            num_scalar_prefetch=1,
            grid=(1,),
            in_specs=[pl.BlockSpec(memory_space=pl.ANY)] * 9,
            out_specs=[out_spec, out_spec],
            scratch_shapes=[
                pltpu.VMEM((4, features, depth), jnp.bfloat16),
                pltpu.VMEM((4, tokens, columns), jnp.bfloat16),
                pltpu.SemaphoreType.DMA((4, 2)),
                pltpu.SemaphoreType.DMA((4, 2)),
            ],
        ),
        out_shape=[
            jax.ShapeDtypeStruct((2, rows, columns), jnp.float32),
            jax.ShapeDtypeStruct((2, rows, columns), jnp.bfloat16),
        ],
        compiler_params=limit(mib),
        cost_estimate=brief,
        name="contract",
    )(place, *lefts, own, brought[1], brought[0], *following)


def natural_kernel(place, left, basis, natural):
    natural[...] = dot(left[...], basis[0], ((1,), (1,))).astype(natural.dtype)


def natural_rows(place, left, basis, whose):
    rows, block = left.shape
    tile = block // 2
    return pl.pallas_call(
        natural_kernel,
        grid_spec=pltpu.PrefetchScalarGridSpec(
            num_scalar_prefetch=1,
            grid=(2,),
            in_specs=[
                pl.BlockSpec((rows // 2, block), lambda i, s: (s[0] ^ whose, 0)),
                pl.BlockSpec((1, tile, block), lambda i, s: (s[0], i, 0)),
            ],
            out_specs=pl.BlockSpec((rows // 2, tile), lambda i, s: (0, i)),
        ),
        out_shape=jax.ShapeDtypeStruct((rows // 2, block), jnp.bfloat16),
        compiler_params=limit(24),
        cost_estimate=brief,
        name="natural",
    )(place, left, basis)


def place_kernel(place, own, other, out):
    @pl.when(pl.program_id(0) == place[0])
    def _():
        out[...] = own[...]

    @pl.when(pl.program_id(0) != place[0])
    def _():
        out[...] = other[...]


def side_by_side(place, own, other):
    rows, block = own.shape
    whole = pl.BlockSpec((rows, block), lambda i, s: (0, 0))
    return pl.pallas_call(
        place_kernel,
        grid_spec=pltpu.PrefetchScalarGridSpec(
            num_scalar_prefetch=1,
            grid=(2,),
            in_specs=[whole, whole],
            out_specs=pl.BlockSpec((rows, block), lambda i, s: (0, i)),
        ),
        out_shape=jax.ShapeDtypeStruct((rows, 2 * block), own.dtype),
        compiler_params=limit(24),
        cost_estimate=brief,
        name="side_by_side",
    )(place, own, other)


def shards(activations, out_grads, basis_in, basis_out):
    tokens, half_in = activations.shape
    block = basis_in.shape[1]
    near = block // 2
    x = lax.axis_index("x")
    y = lax.axis_index("y")
    z_lo = lax.axis_index("z_lo")
    z_hi = lax.axis_index("z_hi")
    core = lax.axis_index("core")
    turn = jnp.reshape((x - y) % 4, (1,))
    place = jnp.reshape(core, (1,))

    mine = transpose_xy(activations)
    other_out = swap(partner_columns(place, out_grads, block), "core")
    block_basis = lax.dynamic_index_in_dim(basis_in, x, 0, keepdims=False)
    by_column = jnp.concatenate(
        [lax.dynamic_slice_in_dim(block_basis, k * near, near, 1) for k in (z_hi, 1 - z_hi)], 1
    )
    basis_turn = jnp.concatenate(
        [lax.dynamic_slice_in_dim(by_column, k * half_in, half_in, 0) for k in (z_lo, 1 - z_lo)], 0
    ).T
    basis_rows = lax.dynamic_slice_in_dim(by_column, z_hi * near, near, 0)
    own_out = rotated_out(place, out_grads, other_out, basis_out)

    def around_x(right, left):
        return [along_x(right, 1), along_x(left, -1)]

    mine, basis_turn, basis_rows, *own_out = fence(mine, basis_turn, basis_rows, *own_out)
    columns = own_out[0].shape[1]

    other = swap(mine, "z_lo")
    two = along_y(mine, 2)
    first = around_x(own_out[0], own_out[0])
    mine, other, two = fence(mine, other, two)

    whole = jnp.concatenate([mine, other], 1)
    below, above = along_y(whole, 1), along_y(whole, -1)
    second = around_x(*payloads(own_out[1], columns, *first))
    two = jnp.concatenate([two, swap(two, "z_lo")], 1)
    early = rotated(basis_turn, whole, two)
    below, above, early, *second = fence(below, above, early, *second)

    def finished(kept, got):
        total = kept + got.astype(jnp.float32)
        tokens_all = tokens * 16
        scales = total[0] / tokens_all
        turned = (total[1] / math.sqrt(tokens_all) / (scales + damping)).astype(jnp.bfloat16)
        return scales, turned

    def product(turned, over):
        total = dot(basis_rows[:, :near], turned) + dot(basis_rows[:, near:], over)
        return total.astype(jnp.bfloat16)

    third = around_x(*payloads(own_out[2], columns, *second))
    late = rotated(basis_turn, above, below)
    lefts = [early, swap(early, "core"), late, swap(late, "core")]
    kept0, send0 = contracted(turn, lefts, own_out[0], first, second, 0, 53)
    own0, send0 = fence(own_out[0], send0)
    kept0b, send0b = contracted(turn, lefts, own0, first, second, 1, 53)
    got0, got0b = swap(send0, "z_hi"), swap(send0b, "z_hi")
    *third, send0b = fence(*third, send0b)
    fourth = around_x(*payloads(own_out[3], columns, *third))
    own1, got0 = fence(own_out[1], got0)
    kept1, send1 = contracted(turn, lefts, own1, second, third)
    got1 = swap(send1, "z_hi")
    scales0, turned0 = finished(kept0, got0)
    scales0b, turned0b = finished(kept0b, got0b)
    scales0 = jnp.concatenate([scales0, scales0b], 1)
    turned0 = jnp.concatenate([turned0, turned0b], 1)
    over0 = swap(turned0, "z_hi")
    *fourth, send1 = fence(*fourth, send1)
    fifth = around_x(*payloads(None, columns, *fourth, mib=60))
    kept2, send2 = contracted(turn, lefts, own_out[2], third, fourth)
    got2 = swap(send2, "z_hi")
    *fifth, send2, got1, over0 = fence(*fifth, send2, got1, over0)
    kept3, send3 = contracted(turn, lefts, own_out[3], fourth, fifth)

    got3 = swap(send3, "z_hi")
    got1, _ = fence(got1, send3)
    done = [(scales0, turned0)] + [finished(*pair) for pair in ((kept1, got1), (kept2, got2), (kept3, got3))]
    left01 = product(turned0, over0)
    left12 = product(done[1][1], swap(done[1][1], "z_hi"))
    left2 = product(done[2][1], swap(done[2][1], "z_hi"))
    over3 = swap(done[3][1], "z_hi")
    scales = jnp.concatenate([scale for scale, _ in done], 1)
    quarter = near // 2
    scales_own = lax.dynamic_slice_in_dim(scales, core * quarter, quarter, 0)
    scales_other = swap(lax.dynamic_slice_in_dim(scales, (1 - core) * quarter, quarter, 0), "core")
    scales = side_by_side(place, scales_own, scales_other)
    over3, left2, left12, left01, scales = fence(over3, left2, left12, left01, scales)
    left = jnp.concatenate([left01, left12, left2, product(done[3][1], over3)], 1)
    natural_other = swap(natural_rows(place, left, basis_out, 1), "core")
    natural = side_by_side(place, natural_rows(place, left, basis_out, 0), natural_other)
    return scales, natural


def solution(mesh):
    split = Mesh(mesh.devices.reshape(4, 2, 2, 4, 2), ("x", "z_hi", "core", "y", "z_lo"))
    dp, tensor = ("x", "z_hi", "core"), ("y", "z_lo")
    return jax.shard_map(
        shards,
        mesh=split,
        in_specs=(P(dp, tensor), P(dp, tensor), P(), P(tensor, None, None)),
        out_specs=(P(dp, tensor), P(dp, tensor)),
        check_vma=False,
    )
```
